128 devices in a mesh: dp: 32 (over z, x_lo, y), pair: 4 (over x_hi, core).
Axes of the slice: x: 4 (x_hi: 2, x_lo: 2; x = x_hi * 2 + x_lo), y: 4, z: 4, core: 2. Of those that a mesh axis runs over, the one named last changes fastest.
Arguments:
- protein: float32 [16384, 1024], P(('dp', 'pair')), may hold values from -6 to 6
- text: float32 [16384, 1024], P(('dp', 'pair')), may hold values from -6 to 6
- scale: float32 [], replicated, may hold values from 5 to 15
- bias: float32 [], replicated, may hold values from -4 to -2
Outputs:
- grad_protein: float32 [16384, 1024], P(('dp', 'pair'))
- grad_text: float32 [16384, 1024], P(('dp', 'pair'))
The draws below stay inside these ranges and needn't reach their ends.
All inputs are finite; a program needn't handle non-finite values.
Results may differ from the reference program's by a relative error of at most 0.006.
Values may be sent and summed in bfloat16 or wider, within the bound.
A program may use at most 64 MiB of HBM per device.

```python
import math
import jax
import jax.numpy as jnp
from jax import lax

D = 1024
N = 16384


def block_levels(own_key, shape, shards, smallest, high):
    level = 1.0
    for dim, parts in shards:
        steps = jax.random.uniform(jax.random.fold_in(jax.random.fold_in(own_key, 6), dim), (parts,), jnp.float32, smallest / len(shards), high / len(shards))
        level = level * jnp.repeat(jnp.exp(steps), shape[dim] // parts).reshape((-1,) + (1,) * (len(shape) - 1 - dim))
    return level


def gaussian(own_key, shape, scale, limit, shards=(), kind=jnp.bfloat16):
    gain = block_levels(own_key, shape, shards, -0.22, 0.18) if shards else 1.0
    entries = jax.random.normal(own_key, shape, jnp.float32) * scale * gain
    return jnp.minimum(jnp.maximum(entries, -limit), limit).astype(kind)


def setup_inputs(seed: int = 0) -> dict:
    streams_of = jax.random.split(jax.random.key(seed), 5)
    protein = gaussian(streams_of[0], (N, D), 1.0, 6.0, ((0, 128),), jnp.float32)
    text = gaussian(streams_of[1], (N, D), 1.0, 6.0, ((0, 128),), jnp.float32)
    scale = jnp.clip(jnp.exp(jax.random.uniform(streams_of[2], (), jnp.float32, math.log(5.0), math.log(15.0))), 5.0, 15.0)
    bias = jnp.clip(jax.random.uniform(streams_of[3], (), jnp.float32, -4.0, -2.0), -4.0, -2.0)
    return {"protein": protein, "text": text, "scale": scale, "bias": bias}


def unit_rows(values):
    norm = jnp.sqrt(lax.optimization_barrier(jnp.sum(values * values, axis=1, keepdims=True)) + 1e-06)
    return (values / norm, norm)

def back_norm(grad_unit, unit, norm):
    inner = lax.optimization_barrier(jnp.sum(unit * grad_unit, axis=1, keepdims=True))
    return (grad_unit - unit * inner) / norm

def reference(protein, text, scale, bias):
    unit_p, norm_p = unit_rows(protein)
    unit_q, norm_q = unit_rows(text)
    unit_pb = unit_p.astype(jnp.bfloat16)
    unit_qb = unit_q.astype(jnp.bfloat16)
    block = min(512, N)
    count = N // block
    cols = jnp.arange(N, dtype=jnp.int32)

    def step(carry, index):
        start = (index * block).astype(jnp.int32)
        rows_b = lax.dynamic_slice_in_dim(unit_pb, start, block, 0)
        logit = scale * jnp.dot(rows_b, unit_qb.T, preferred_element_type=jnp.float32) + bias
        rows = start + jnp.arange(block, dtype=jnp.int32)
        sign = jnp.where(rows[:, None] == cols[None, :], 1.0, -1.0).astype(jnp.float32)
        coef = (-sign * jax.nn.sigmoid(-sign * logit) * scale).astype(jnp.bfloat16)
        grad_rows = jnp.dot(coef, unit_qb, preferred_element_type=jnp.float32)
        carry = carry + jnp.dot(coef.T, rows_b, preferred_element_type=jnp.float32)
        return (carry, grad_rows)
    grad_unit_q, grad_blocks = lax.scan(step, jnp.zeros((N, D), jnp.float32), jnp.arange(count, dtype=jnp.int32))
    grad_unit_p = grad_blocks.reshape(N, D)
    return (back_norm(grad_unit_p, unit_p, norm_p), back_norm(grad_unit_q, unit_q, norm_q))
```

```python
import math

import jax
import jax.numpy as jnp
from jax import lax
from jax.experimental import pallas as pl
from jax.experimental.pallas import tpu as pltpu
from jax.sharding import PartitionSpec as P

MESH = pl.DeviceIdType.MESH
F32, BF16 = jnp.float32, jnp.bfloat16
LOG2E = math.log2(math.e)
WIDTH = 1024
ROWS = 128
BLOCK = 256
PARTS = ((0, 48, 0), (48, 48, 96), (96, 32, 192))
N_COPIES = 56


def neighbours():
    dp, pair = lax.axis_index("dp"), lax.axis_index("pair")
    z, x_lo, y = dp // 8, (dp // 4) % 2, dp % 4
    x_hi, core = pair // 2, pair % 2
    x = x_hi * 2 + x_lo

    def device(x, y, z, core):
        return (z * 8 + (x % 2) * 4 + y, (x // 2) * 2 + core)

    def p_flip(i):
        return i + 1 - 2 * (i % 2)

    def q_flip(i):
        return (i + 3 + 2 * (i % 2)) % 4

    def cube(flip):
        return (device(flip(x), y, z, core), device(x, flip(y), z, core), device(x, y, flip(z), core))

    return cube(p_flip), cube(q_flip), device(x, y, z, 1 - core)


def kernel(
    scale_ref, bias_ref, protein, text, out_p, out_q,
    unit_p, unit_q, norm_p, norm_q, rows_p, rows_q, coef, acc_p, acc_q, sib_out, sib_in,
    out1_p, out1_q, in1_p, in1_q, out2_p, out2_q, in2_p, in2_q, out3_p, out3_q, in3_p, in3_q,
    load_sem, send_sem, recv_sem,
):
    cube_p, cube_q, sibling = neighbours()
    barrier = pltpu.get_barrier_semaphore()
    for device in (*cube_p, *cube_q, sibling):
        pl.semaphore_signal(barrier, inc=1, device_id=device, device_id_type=MESH)
    load_p = pltpu.make_async_copy(protein, unit_p, load_sem.at[0])
    load_q = pltpu.make_async_copy(text, unit_q, load_sem.at[1])
    load_p.start()
    load_q.start()
    scale, bias = scale_ref[0], bias_ref[0]
    copies = []

    def send(src, dst, device):
        i = len(copies)
        copy = pltpu.make_async_remote_copy(
            src_ref=src, dst_ref=dst, send_sem=send_sem.at[i], recv_sem=recv_sem.at[i],
            device_id=device, device_id_type=MESH,
        )
        copy.start()
        copies.append(copy)
        return copy

    def normalise(load, unit, norm, rows):
        load.wait()
        values = unit[...]
        length = jnp.sqrt(jnp.sum(values * values, axis=1, keepdims=True) + 1e-06)
        values = values / length
        unit[...] = values
        norm[...] = length
        for first, size, offset in PARTS:
            rows[offset : offset + size, :] = values[first : first + size].astype(BF16)

    normalise(load_p, unit_p, norm_p, rows_p)
    normalise(load_q, unit_q, norm_q, rows_q)
    pl.semaphore_wait(barrier, 7)

    sides = ((rows_p, 512, cube_p), (rows_q, 256, cube_q))

    def gather(side, part, source, target, link):
        rows, stride, cube = sides[side]
        _, size, offset = PARTS[part]
        return send(
            rows.at[pl.ds(source * stride + offset, 2 * size)],
            rows.at[pl.ds(target * stride + offset, 2 * size)],
            cube[(part + link) % 3],
        )

    def to_sibling(block):
        return send(
            rows_p.at[pl.ds(block * 512, BLOCK)], rows_p.at[pl.ds(block * 512 + BLOCK, BLOCK)], sibling
        )

    both = [(side, part) for part in range(3) for side in range(2)]
    first = {}
    for side, part in both:
        rows, _, cube = sides[side]
        _, size, offset = PARTS[part]
        first[side, part] = send(
            rows.at[pl.ds(offset, size)], rows.at[pl.ds(offset + size, size)], cube[part]
        )
    second, third, fourth, siblings = {}, {}, {}, {}
    for side, part in both:
        first[side, part].wait_recv()
        second[side, part] = gather(side, part, 0, 1, 1)
    for side, part in both:
        third[side, part] = gather(side, part, 0, 2, 2)
    siblings[0] = to_sibling(0)

    def logits(row, size, block):
        return lax.dot_general(
            rows_p[row : row + size, :], rows_q[block * BLOCK : (block + 1) * BLOCK, :],
            (((1,), (1,)), ((), ())), preferred_element_type=F32,
        )

    slope, shift = scale * -LOG2E, bias * -LOG2E

    def fill(row, size, block):
        power = jnp.exp2(logits(row, size, block) * slope + shift)
        coef[row : row + size, block * BLOCK : (block + 1) * BLOCK] = (scale / (1.0 + power)).astype(BF16)

    def fill_own():
        values = scale * logits(0, BLOCK, 0) + bias
        row = lax.broadcasted_iota(jnp.int32, (BLOCK, BLOCK), 0)
        column = lax.broadcasted_iota(jnp.int32, (BLOCK, BLOCK), 1)
        own = (row < 48) | ((row >= 96) & (row < 144)) | ((row >= 192) & (row < 224))
        sign = jnp.where((row == column) & own, 1.0, -1.0)
        coef[0:BLOCK, 0:BLOCK] = (-sign * scale / (1.0 + jnp.exp2(sign * values * LOG2E))).astype(BF16)

    fill_own()
    siblings[0].wait_recv()
    fill(BLOCK, BLOCK, 0)
    for side, part in both:
        second[side, part].wait_recv()
        fourth[side, part] = gather(side, part, 1, 3, 2)
    siblings[1] = to_sibling(1)
    for block, arrivals in ((1, None), (2, third), (3, fourth)):
        if arrivals is not None:
            for side, part in both:
                arrivals[side, part].wait_recv()
            siblings[block] = to_sibling(block)
        for start in range(0, block * 512, 1024):
            fill(start, min(1024, block * 512 - start), block)
        siblings[block].wait_recv()
        for column in range(block + 1):
            fill(block * 512, 512, column)

    def grad_p(block, half):
        row = block * 512 + half * BLOCK
        return jnp.dot(coef[row : row + BLOCK, :], rows_q[...], preferred_element_type=F32)

    def grad_q(block):
        return lax.dot_general(
            coef[:, block * BLOCK : (block + 1) * BLOCK], rows_p[...],
            (((0,), (0,)), ((), ())), preferred_element_type=F32,
        )

    sib_sums = {}

    def give_sibling(block):
        rows = pl.ds(block * BLOCK, BLOCK)
        sib_out[rows, :] = grad_p(block, 1)
        sib_sums[block] = send(sib_out.at[rows], sib_in.at[rows], sibling)

    def own_p(block):
        own = grad_p(block, 0)
        sib_sums[block].wait_recv()
        return own + sib_in[pl.ds(block * BLOCK, BLOCK), :]

    def halve(value, out, landing, block, cube):
        start = (block - 2) * BLOCK
        out[pl.ds(start, BLOCK), :] = value.astype(BF16)
        sent = []
        for part, (_, size, offset) in enumerate(PARTS):
            rows = pl.ds(start + offset, 2 * size)
            sent.append(send(out.at[rows], landing.at[rows], cube[(part + 2) % 3]))
        return sent

    sums1 = {}
    for block in (3, 2):
        give_sibling(block)
        sums1[1, block] = halve(grad_q(block), out1_q, in1_q, block, cube_q)
        sums1[0, block] = halve(own_p(block), out1_p, in1_p, block, cube_p)

    def halve_again(side, acc, landed, out, landing, cube):
        for copy in sums1[side, 3]:
            copy.wait_recv()
        out[...] = (acc[pl.ds(BLOCK, BLOCK), :] + landed[pl.ds(BLOCK, BLOCK), :].astype(F32)).astype(BF16)
        sent = []
        for part, (_, size, offset) in enumerate(PARTS):
            rows = pl.ds(offset, 2 * size)
            sent.append(send(out.at[rows], landing.at[rows], cube[(part + 1) % 3]))
        return sent

    give_sibling(1)
    acc_q[pl.ds(BLOCK, BLOCK), :] = grad_q(1)
    acc_p[pl.ds(BLOCK, BLOCK), :] = own_p(1)
    sums2 = {}
    sums2[1] = halve_again(1, acc_q, in1_q, out2_q, in2_q, cube_q)
    sums2[0] = halve_again(0, acc_p, in1_p, out2_p, in2_p, cube_p)
    give_sibling(0)
    acc_q[pl.ds(0, BLOCK), :] = grad_q(0)
    acc_p[pl.ds(0, BLOCK), :] = own_p(0)

    ends = (
        (1, acc_q, in1_q, in2_q, out3_q, in3_q, cube_q, unit_q, norm_q, out_q),
        (0, acc_p, in1_p, in2_p, out3_p, in3_p, cube_p, unit_p, norm_p, out_p),
    )
    sums3 = {}
    for side, acc, in1, in2, out3, in3, cube, _, _, _ in ends:
        for part, (first_row, size, offset) in enumerate(PARTS):
            sums1[side, 2][part].wait_recv()
            sums2[side][part].wait_recv()
            rows = pl.ds(offset, 2 * size)
            total = acc[rows, :] + in1[rows, :].astype(F32) + in2[rows, :].astype(F32)
            acc[rows, :] = total
            mine = pl.ds(first_row, size)
            out3[mine, :] = total[size:].astype(BF16)
            sums3[side, part] = send(out3.at[mine], in3.at[mine], cube[part])
    for side, acc, _, _, _, in3, _, unit, norm, out in ends:
        for part, (first_row, size, offset) in enumerate(PARTS):
            sums3[side, part].wait_recv()
            mine = pl.ds(first_row, size)
            grad = acc[pl.ds(offset, size), :] + in3[mine, :].astype(F32)
            direction = unit[mine, :]
            inner = jnp.sum(direction * grad, axis=1, keepdims=True)
            out[mine, :] = (grad - direction * inner) / norm[mine, :]
    for copy in copies:
        copy.wait_send()


def on_device(protein, text, scale, bias):
    def buffer(rows, kind):
        return pltpu.VMEM((rows, WIDTH), kind)

    result = jax.ShapeDtypeStruct((ROWS, WIDTH), F32)
    return pl.pallas_call(
        kernel,
        out_shape=(result, result),
        in_specs=[pl.BlockSpec(memory_space=pltpu.SMEM)] * 2 + [pl.BlockSpec(memory_space=pl.ANY)] * 2,
        out_specs=[pl.BlockSpec(memory_space=pltpu.VMEM)] * 2,
        scratch_shapes=[
            buffer(ROWS, F32), buffer(ROWS, F32), pltpu.VMEM((ROWS, 1), F32), pltpu.VMEM((ROWS, 1), F32),
            buffer(2048, BF16), buffer(1024, BF16), buffer(2048, BF16),
            buffer(512, F32), buffer(512, F32), buffer(1024, F32), buffer(1024, F32),
            buffer(512, BF16), buffer(512, BF16), buffer(512, BF16), buffer(512, BF16),
            buffer(256, BF16), buffer(256, BF16), buffer(256, BF16), buffer(256, BF16),
            buffer(128, BF16), buffer(128, BF16), buffer(128, BF16), buffer(128, BF16),
            pltpu.SemaphoreType.DMA((2,)),
            pltpu.SemaphoreType.DMA((N_COPIES,)),
            pltpu.SemaphoreType.DMA((N_COPIES,)),
        ],
        compiler_params=pltpu.CompilerParams(
            collective_id=0, has_side_effects=True, vmem_limit_bytes=56 * 1024 * 1024
        ),
    )(scale.reshape(1), bias.reshape(1), protein, text)


def solution(mesh):
    in_specs = (P(("dp", "pair"), None), P(("dp", "pair"), None), P(), P())
    out_specs = (P(("dp", "pair"), None), P(("dp", "pair"), None))
    return jax.shard_map(on_device, mesh=mesh, in_specs=in_specs, out_specs=out_specs, check_vma=False)
```

```python
import math

import jax
import jax.numpy as jnp
from jax import lax
from jax.experimental import pallas as pl
from jax.experimental.pallas import tpu as pltpu
from jax.sharding import PartitionSpec as P

MESH = pl.DeviceIdType.MESH
F32, BF16 = jnp.float32, jnp.bfloat16
LOG2E = math.log2(math.e)
WIDTH = 1024
ROWS = 128
PARTS = ((0, 48), (48, 48), (96, 32))
PLACE = (0, 1, 2, 4, 3, 5, 6, 7)
N_COPIES = 114


def neighbours():
    dp, pair = lax.axis_index("dp"), lax.axis_index("pair")
    z, x_lo, y = dp // 8, (dp // 4) % 2, dp % 4
    x_hi, core = pair // 2, pair % 2
    x = x_hi * 2 + x_lo

    def device(x, y, z, core):
        return (z * 8 + (x % 2) * 4 + y, (x // 2) * 2 + core)

    def p_flip(i):
        return i + 1 - 2 * (i % 2)

    def q_flip(i):
        return (i + 3 + 2 * (i % 2)) % 4

    def cube(flip):
        dy, dz = flip(y) - y, flip(z) - z
        return (
            device(flip(x), y, z, core),
            device(x, y + (1 - core) * dy, z + core * dz, core),
            device(x, y + core * dy, z + (1 - core) * dz, core),
        )

    return cube(p_flip), cube(q_flip), device(x, y, z, 1 - core)


def kernel(
    scale_ref, bias_ref, protein, text, out_p, out_q,
    unit_p, unit_q, norm_p, norm_q, rows_p, rows_q, coef, early_p, early_q, acc_p, acc_q, own_out, sib_out, sib_in,
    out1_p, out1_q, in1_p, in1_q, out2_p, out2_q, in2_p, in2_q, out3_p, out3_q, in3_p, in3_q,
    load_sem, send_sem, recv_sem,
):
    cube_p, cube_q, sibling = neighbours()
    barrier = pltpu.get_barrier_semaphore()
    for device in (*cube_p, *cube_q, sibling):
        pl.semaphore_signal(barrier, inc=1, device_id=device, device_id_type=MESH)
    load_p = pltpu.make_async_copy(protein, unit_p, load_sem.at[0])
    load_q = pltpu.make_async_copy(text, unit_q, load_sem.at[1])
    load_p.start()
    load_q.start()
    scale, bias = scale_ref[0], bias_ref[0]
    copies = []

    def send(src, dst, device):
        i = len(copies)
        copy = pltpu.make_async_remote_copy(
            src_ref=src, dst_ref=dst, send_sem=send_sem.at[i], recv_sem=recv_sem.at[i],
            device_id=device, device_id_type=MESH,
        )
        copy.start()
        copies.append(copy)
        return copy

    def normalise(load, unit, norm, rows):
        load.wait()
        values = unit[...]
        length = jnp.sqrt(jnp.sum(values * values, axis=1, keepdims=True) + 1e-06)
        values = values / length
        unit[...] = values
        norm[...] = length
        rows[0:ROWS, :] = values.astype(BF16)

    normalise(load_p, unit_p, norm_p, rows_p)
    normalise(load_q, unit_q, norm_q, rows_q)
    pl.semaphore_wait(barrier, 7)

    sides = ((rows_p, 2 * ROWS, cube_p), (rows_q, ROWS, cube_q))
    both = [(side, part) for part in range(3) for side in range(2)]
    arrival, from_sibling = {}, {}

    def pass_on(slot, link):
        for side, part in both:
            pass_part(side, part, slot, link)

    def pass_part(side, part, slot, link):
        rows, stride, cube = sides[side]
        start, size = PARTS[part]
        target = slot + (1 << link)
        arrival[side, part, target] = send(
            rows.at[pl.ds(PLACE[slot] * stride + start, size)],
            rows.at[pl.ds(PLACE[target] * stride + start, size)],
            cube[(part + link) % 3],
        )

    def to_sibling(place, start, size):
        row = place * 2 * ROWS + start
        from_sibling.setdefault(place, []).append(
            send(rows_p.at[pl.ds(row, size)], rows_p.at[pl.ds(row + ROWS, size)], sibling)
        )

    def receive(slot, links=()):
        for side, part in both:
            arrival[side, part, slot].wait_recv()
            if side == 0:
                to_sibling(PLACE[slot], *PARTS[part])
            for link in links[:1]:
                pass_part(side, part, slot, link)
        for link in links[1:]:
            pass_on(slot, link)

    def receive_sibling(*places):
        for place in places:
            for copy in from_sibling[place]:
                copy.wait_recv()

    slope, shift = scale * -LOG2E, bias * -LOG2E

    def dots(row, size, column, width):
        return lax.dot_general(
            rows_p[row : row + size, :], rows_q[column : column + width, :],
            (((1,), (1,)), ((), ())), preferred_element_type=F32,
        )

    def fill(row, end, column, last):
        power = jnp.exp2(dots(row, end - row, column, last - column) * slope + shift)
        coef[row:end, column:last] = (scale / (1.0 + power)).astype(BF16)

    def fill_own():
        values = dots(0, 4 * ROWS, 0, 2 * ROWS) * -slope - shift
        row = lax.broadcasted_iota(jnp.int32, values.shape, 0)
        column = lax.broadcasted_iota(jnp.int32, values.shape, 1)
        sign = jnp.where((row == column) & (row < ROWS), 1.0, -1.0)
        coef[0 : 4 * ROWS, 0 : 2 * ROWS] = (-sign * scale / (1.0 + jnp.exp2(sign * values))).astype(BF16)

    for link in range(3):
        pass_on(0, link)
    to_sibling(0, 0, ROWS)
    receive(1, (1, 2))
    receive(2, (2,))
    receive_sibling(0, 1)
    fill_own()
    receive(4)
    receive(3, (2,))
    receive_sibling(2, 3)
    fill(0, 512, 256, 512)
    fill(512, 1024, 0, 512)
    receive(5)
    fill(0, 1024, 512, 768)
    receive_sibling(4, 5)
    fill(1024, 1536, 0, 768)

    def grad_p(place, start=0, end=8 * ROWS):
        row = place * 2 * ROWS
        return jnp.dot(coef[row : row + 2 * ROWS, start:end], rows_q[start:end, :], preferred_element_type=F32)

    def grad_q(place, start=0, end=16 * ROWS):
        return lax.dot_general(
            coef[start:end, place * ROWS : (place + 1) * ROWS], rows_p[start:end, :],
            (((0,), (0,)), ((), ())), preferred_element_type=F32,
        )

    sib_sums, sums = {}, {}

    def share(place, value):
        rows = pl.ds(place * ROWS, ROWS)
        sib_out[rows, :] = value[ROWS:]
        sib_sums[place] = send(sib_out.at[rows], sib_in.at[rows], sibling)
        own_out[rows, :] = value[:ROWS]

    def own_p(place):
        rows = pl.ds(place * ROWS, ROWS)
        sib_sums[place].wait_recv()
        return own_out[rows, :] + sib_in[rows, :]

    accs = (acc_p, acc_q)
    outs = ((out3_p, out2_p, out1_p), (out3_q, out2_q, out1_q))
    ins = ((in3_p, in2_p, in1_p), (in3_q, in2_q, in1_q))
    cubes = (cube_p, cube_q)

    def give(side, slot, part):
        link = slot.bit_length() - 1
        start, size = PARTS[part]
        rows = pl.ds((slot - (1 << link)) * ROWS + start, size)
        sums[side, slot, part] = send(
            outs[side][link].at[rows], ins[side][link].at[rows], cubes[side][(part + link) % 3]
        )

    def put(side, slot, value):
        link = slot.bit_length() - 1
        outs[side][link][pl.ds((slot - (1 << link)) * ROWS, ROWS), :] = value.astype(BF16)

    def give_all(side, slot):
        for part in range(3):
            give(side, slot, part)

    def total(side, slot, part):
        start, size = PARTS[part]
        rows = pl.ds(slot * ROWS + start, size)
        value = accs[side][rows, :]
        for link in (2, 1, 0):
            if slot < 1 << link:
                sums[side, slot + (1 << link), part].wait_recv()
                value += ins[side][link][rows, :].astype(F32)
        return value

    def add_and_give(side, slot):
        link = slot.bit_length() - 1
        for part, (start, size) in enumerate(PARTS):
            rows = pl.ds((slot - (1 << link)) * ROWS + start, size)
            outs[side][link][rows, :] = total(side, slot, part).astype(BF16)
            give(side, slot, part)

    def keep(side, slot, value):
        accs[side][pl.ds(slot * ROWS, ROWS), :] = value

    def give_p(slot):
        put(0, slot, own_p(PLACE[slot]))
        give_all(0, slot)

    def give_q(slot):
        put(1, slot, grad_q(PLACE[slot]))
        give_all(1, slot)

    early_p[...] = grad_p(5, 0, 768)
    receive(6)
    receive_sibling(6)
    fill(1536, 1792, 0, 768)
    early_q[...] = grad_q(5, 0, 1792)
    receive(7)
    fill(1280, 1536, 768, 1024)
    share(5, early_p[...] + grad_p(5, 768, 1024))
    fill(0, 1024, 768, 1024)
    receive_sibling(7)
    fill(1792, 2048, 0, 1024)
    put(1, 5, early_q[...] + grad_q(5, 1792, 2048))
    give_all(1, 5)
    share(7, grad_p(7))
    give_p(5)
    fill(1024, 1280, 768, 1024)
    fill(1536, 1792, 768, 1024)
    give_q(7)
    share(6, grad_p(6))
    give_p(7)
    give_q(6)
    share(4, grad_p(4))
    give_p(6)
    keep(1, 3, grad_q(4))
    share(3, grad_p(3))
    put(1, 4, grad_q(3))
    keep(0, 3, own_p(4))
    for side in (1, 0):
        add_and_give(side, 3)
    give_all(1, 4)
    give_p(4)
    share(2, grad_p(2))
    keep(1, 2, grad_q(2))
    share(1, grad_p(1))
    keep(0, 2, own_p(2))
    for side in (1, 0):
        add_and_give(side, 2)
    keep(1, 1, grad_q(1))
    share(0, grad_p(0))
    keep(0, 1, own_p(1))
    keep(1, 0, grad_q(0))
    keep(0, 0, own_p(0))
    for side in (1, 0):
        add_and_give(side, 1)
    for side, unit, norm, out in ((1, unit_q, norm_q, out_q), (0, unit_p, norm_p, out_p)):
        for part, (start, size) in enumerate(PARTS):
            rows = pl.ds(start, size)
            grad = total(side, 0, part)
            direction = unit[rows, :]
            inner = jnp.sum(direction * grad, axis=1, keepdims=True)
            out[rows, :] = (grad - direction * inner) / norm[rows, :]
    for copy in copies:
        copy.wait_send()


def on_device(protein, text, scale, bias):
    def buffer(rows, kind):
        return pltpu.VMEM((rows, WIDTH), kind)

    result = pltpu.VMEM((ROWS, WIDTH), F32)
    return pl.pallas_call(
        kernel,
        out_shape=(result, result),
        in_specs=[pl.BlockSpec(memory_space=pltpu.SMEM)] * 2 + [pl.BlockSpec(memory_space=pl.ANY)] * 2,
        out_specs=[pl.BlockSpec(memory_space=pltpu.VMEM)] * 2,
        scratch_shapes=[
            buffer(ROWS, F32), buffer(ROWS, F32), pltpu.VMEM((ROWS, 1), F32), pltpu.VMEM((ROWS, 1), F32),
            buffer(2048, BF16), buffer(1024, BF16), buffer(2048, BF16),
            buffer(2 * ROWS, F32), buffer(ROWS, F32),
            *(buffer(4 * ROWS, F32) for _ in range(2)),
            *(buffer(8 * ROWS, F32) for _ in range(3)),
            *(buffer(4 * ROWS, BF16) for _ in range(4)),
            *(buffer(2 * ROWS, BF16) for _ in range(4)),
            *(buffer(ROWS, BF16) for _ in range(4)),
            pltpu.SemaphoreType.DMA((2,)),
            pltpu.SemaphoreType.DMA((N_COPIES,)),
            pltpu.SemaphoreType.DMA((N_COPIES,)),
        ],
        compiler_params=pltpu.CompilerParams(
            collective_id=0, has_side_effects=True, vmem_limit_bytes=56 * 1024 * 1024
        ),
    )(scale.reshape(1), bias.reshape(1), protein, text)


def solution(mesh):
    in_specs = (P(("dp", "pair"), None), P(("dp", "pair"), None), P(), P())
    out_specs = (P(("dp", "pair"), None), P(("dp", "pair"), None))
    return jax.shard_map(on_device, mesh=mesh, in_specs=in_specs, out_specs=out_specs, check_vma=False)
```

```python
import math

import jax
import jax.numpy as jnp
from jax import lax
from jax.experimental import pallas as pl
from jax.experimental.pallas import tpu as pltpu
from jax.sharding import PartitionSpec as P

MESH = pl.DeviceIdType.MESH
F32, BF16 = jnp.float32, jnp.bfloat16
LOG2E = math.log2(math.e)
WIDTH = 1024
ROWS = 128
PARTS = ((0, 48), (48, 48), (96, 32))
PLACE = (0, 1, 2, 4, 3, 5, 6, 7)
N_COPIES = 114
TILE = (256, 256)


def neighbours():
    dp, pair = lax.axis_index("dp"), lax.axis_index("pair")
    z, x_lo, y = dp // 8, (dp // 4) % 2, dp % 4
    x_hi, core = pair // 2, pair % 2
    x = x_hi * 2 + x_lo

    def device(x, y, z, core):
        return (z * 8 + (x % 2) * 4 + y, (x // 2) * 2 + core)

    def p_flip(i):
        return i + 1 - 2 * (i % 2)

    def q_flip(i):
        return (i + 3 + 2 * (i % 2)) % 4

    def cube(flip):
        dy, dz = flip(y) - y, flip(z) - z
        return (
            device(flip(x), y, z, core),
            device(x, y + (1 - core) * dy, z + core * dz, core),
            device(x, y + core * dy, z + (1 - core) * dz, core),
        )

    return cube(p_flip), cube(q_flip), device(x, y, z, 1 - core)


def kernel(
    scale_ref, bias_ref, protein, text, out_p, out_q,
    unit_p, unit_q, norm_p, norm_q, rows_p, rows_q, coef, early_p, early_q, acc_p, acc_q, own_out, sib_out, sib_in,
    out1_p, out1_q, in1_p, in1_q, out2_p, out2_q, in2_p, in2_q, out3_p, out3_q, in3_p, in3_q,
    load_sem, send_sem, recv_sem,
):
    cube_p, cube_q, sibling = neighbours()
    barrier = pltpu.get_barrier_semaphore()
    for device in (*cube_p, *cube_q, sibling):
        pl.semaphore_signal(barrier, inc=1, device_id=device, device_id_type=MESH)
    load_p = pltpu.make_async_copy(protein, unit_p, load_sem.at[0])
    load_q = pltpu.make_async_copy(text, unit_q, load_sem.at[1])
    load_p.start()
    load_q.start()
    scale, bias = scale_ref[0], bias_ref[0]
    copies = []

    def send(src, dst, device):
        i = len(copies)
        copy = pltpu.make_async_remote_copy(
            src_ref=src, dst_ref=dst, send_sem=send_sem.at[i], recv_sem=recv_sem.at[i],
            device_id=device, device_id_type=MESH,
        )
        copy.start()
        copies.append(copy)
        return copy

    def normalise(load, unit, norm, rows):
        load.wait()
        values = unit[...]
        length = jnp.sqrt(jnp.sum(values * values, axis=1, keepdims=True) + 1e-06)
        values = values / length
        unit[...] = values
        norm[...] = length
        rows[0:ROWS, :] = values.astype(BF16)

    normalise(load_p, unit_p, norm_p, rows_p)
    normalise(load_q, unit_q, norm_q, rows_q)
    pl.semaphore_wait(barrier, 7)

    sides = ((rows_p, 2 * ROWS, cube_p), (rows_q, ROWS, cube_q))
    both = [(side, part) for part in range(3) for side in range(2)]
    arrival, from_sibling = {}, {}

    def pass_on(slot, link):
        for side, part in both:
            pass_part(side, part, slot, link)

    def pass_part(side, part, slot, link):
        rows, stride, cube = sides[side]
        start, size = PARTS[part]
        target = slot + (1 << link)
        arrival[side, part, target] = send(
            rows.at[pl.ds(PLACE[slot] * stride + start, size)],
            rows.at[pl.ds(PLACE[target] * stride + start, size)],
            cube[(part + link) % 3],
        )

    def to_sibling(place, start, size):
        row = place * 2 * ROWS + start
        from_sibling.setdefault(place, []).append(
            send(rows_p.at[pl.ds(row, size)], rows_p.at[pl.ds(row + ROWS, size)], sibling)
        )

    def receive(slot, links=()):
        for side, part in both:
            arrival[side, part, slot].wait_recv()
            if side == 0:
                to_sibling(PLACE[slot], *PARTS[part])
            for link in links[:1]:
                pass_part(side, part, slot, link)
        for link in links[1:]:
            pass_on(slot, link)

    def receive_sibling(*places):
        for place in places:
            for copy in from_sibling[place]:
                copy.wait_recv()

    slope, shift = scale * -LOG2E, bias * -LOG2E

    def dots(row, size, column, width):
        return lax.dot_general(
            rows_p[row : row + size, :], rows_q[column : column + width, :],
            (((1,), (1,)), ((), ())), preferred_element_type=F32,
        )

    def fill(row, end, column, last):
        for left in range(column, last, TILE[1]):
            for top in range(row, end, TILE[0]):
                power = jnp.exp2(dots(top, TILE[0], left, TILE[1]) * slope + shift)
                coef[top : top + TILE[0], left : left + TILE[1]] = (scale / (1.0 + power)).astype(BF16)

    def fill_own():
        values = dots(0, 4 * ROWS, 0, 2 * ROWS) * -slope - shift
        row = lax.broadcasted_iota(jnp.int32, values.shape, 0)
        column = lax.broadcasted_iota(jnp.int32, values.shape, 1)
        sign = jnp.where((row == column) & (row < ROWS), 1.0, -1.0)
        coef[0 : 4 * ROWS, 0 : 2 * ROWS] = (-sign * scale / (1.0 + jnp.exp2(sign * values))).astype(BF16)

    for link in range(3):
        pass_on(0, link)
    to_sibling(0, 0, ROWS)
    receive(1, (1, 2))
    receive(2, (2,))
    receive_sibling(0, 1)
    fill_own()
    receive(4)
    fill(0, 512, 256, 512)
    receive(3, (2,))
    receive_sibling(2, 3)
    fill(512, 1024, 0, 512)
    receive(5)
    def grad_p(place, start=0, end=8 * ROWS):
        row = place * 2 * ROWS
        return jnp.dot(coef[row : row + 2 * ROWS, start:end], rows_q[start:end, :], preferred_element_type=F32)

    def grad_q(place, start=0, end=16 * ROWS):
        return lax.dot_general(
            coef[start:end, place * ROWS : (place + 1) * ROWS], rows_p[start:end, :],
            (((0,), (0,)), ((), ())), preferred_element_type=F32,
        )

    sib_sums, sums = {}, {}

    def share(place, value):
        rows = pl.ds(place * ROWS, ROWS)
        sib_out[rows, :] = value[ROWS:]
        sib_sums[place] = send(sib_out.at[rows], sib_in.at[rows], sibling)
        own_out[rows, :] = value[:ROWS]

    def own_p(place):
        rows = pl.ds(place * ROWS, ROWS)
        sib_sums[place].wait_recv()
        return own_out[rows, :] + sib_in[rows, :]

    accs = (acc_p, acc_q)
    outs = ((out3_p, out2_p, out1_p), (out3_q, out2_q, out1_q))
    ins = ((in3_p, in2_p, in1_p), (in3_q, in2_q, in1_q))
    cubes = (cube_p, cube_q)

    def give(side, slot, part):
        link = slot.bit_length() - 1
        start, size = PARTS[part]
        rows = pl.ds((slot - (1 << link)) * ROWS + start, size)
        sums[side, slot, part] = send(
            outs[side][link].at[rows], ins[side][link].at[rows], cubes[side][(part + link) % 3]
        )

    def put(side, slot, value):
        link = slot.bit_length() - 1
        outs[side][link][pl.ds((slot - (1 << link)) * ROWS, ROWS), :] = value.astype(BF16)

    def give_all(side, slot):
        for part in range(3):
            give(side, slot, part)

    def total(side, slot, part):
        start, size = PARTS[part]
        rows = pl.ds(slot * ROWS + start, size)
        value = accs[side][rows, :]
        for link in (2, 1, 0):
            if slot < 1 << link:
                sums[side, slot + (1 << link), part].wait_recv()
                value += ins[side][link][rows, :].astype(F32)
        return value

    def add_and_give(side, slot):
        link = slot.bit_length() - 1
        for part, (start, size) in enumerate(PARTS):
            rows = pl.ds((slot - (1 << link)) * ROWS + start, size)
            outs[side][link][rows, :] = total(side, slot, part).astype(BF16)
            give(side, slot, part)

    def keep(side, slot, value):
        accs[side][pl.ds(slot * ROWS, ROWS), :] = value

    def give_p(slot):
        put(0, slot, own_p(PLACE[slot]))
        give_all(0, slot)

    def give_q(slot):
        put(1, slot, grad_q(PLACE[slot]))
        give_all(1, slot)

    def both_places(place, store_q):
        value = grad_p(place)
        store_q(grad_q(place))
        share(place, value)

    fill(0, 1024, 512, 768)
    receive_sibling(4)
    fill(1024, 1280, 0, 768)
    receive_sibling(5)
    fill(1280, 1536, 0, 768)
    receive(6)
    early_p[...] = grad_p(5, 0, 768)
    early_q[...] = grad_q(5, 0, 1536)
    receive_sibling(6)
    fill(1536, 1792, 0, 768)
    early_q[...] += grad_q(5, 1536, 1792)
    receive(7)
    fill(1280, 1536, 768, 1024)
    share(5, early_p[...] + grad_p(5, 768, 1024))
    fill(0, 1024, 768, 1024)
    receive_sibling(7)
    fill(1792, 2048, 0, 1024)
    put(1, 5, early_q[...] + grad_q(5, 1792, 2048))
    give_all(1, 5)
    share(7, grad_p(7))
    give_p(5)
    fill(1024, 1280, 768, 1024)
    fill(1536, 1792, 768, 1024)
    give_q(7)
    give_p(7)
    share(6, grad_p(6))
    give_q(6)
    both_places(4, lambda value: keep(1, 3, value))
    give_p(6)
    both_places(3, lambda value: put(1, 4, value))
    keep(1, 2, grad_q(2))
    add_and_give(1, 3)
    give_all(1, 4)
    share(2, grad_p(2))
    keep(0, 3, own_p(4))
    add_and_give(0, 3)
    give_p(4)
    both_places(1, lambda value: keep(1, 1, value))
    add_and_give(1, 2)
    keep(0, 2, own_p(2))
    add_and_give(0, 2)
    both_places(0, lambda value: keep(1, 0, value))
    add_and_give(1, 1)
    keep(0, 1, own_p(1))
    keep(0, 0, own_p(0))
    add_and_give(0, 1)
    for side, unit, norm, out in ((1, unit_q, norm_q, out_q), (0, unit_p, norm_p, out_p)):
        for part, (start, size) in enumerate(PARTS):
            rows = pl.ds(start, size)
            grad = total(side, 0, part)
            direction = unit[rows, :]
            inner = jnp.sum(direction * grad, axis=1, keepdims=True)
            out[rows, :] = (grad - direction * inner) / norm[rows, :]
    for copy in copies:
        copy.wait_send()


def on_device(protein, text, scale, bias):
    def buffer(rows, kind):
        return pltpu.VMEM((rows, WIDTH), kind)

    result = pltpu.VMEM((ROWS, WIDTH), F32)
    return pl.pallas_call(
        kernel,
        out_shape=(result, result),
        in_specs=[pl.BlockSpec(memory_space=pltpu.SMEM)] * 2 + [pl.BlockSpec(memory_space=pl.ANY)] * 2,
        out_specs=[pl.BlockSpec(memory_space=pltpu.VMEM)] * 2,
        scratch_shapes=[
            buffer(ROWS, F32), buffer(ROWS, F32), pltpu.VMEM((ROWS, 1), F32), pltpu.VMEM((ROWS, 1), F32),
            buffer(2048, BF16), buffer(1024, BF16), buffer(2048, BF16),
            buffer(2 * ROWS, F32), buffer(ROWS, F32),
            *(buffer(4 * ROWS, F32) for _ in range(2)),
            *(buffer(8 * ROWS, F32) for _ in range(3)),
            *(buffer(4 * ROWS, BF16) for _ in range(4)),
            *(buffer(2 * ROWS, BF16) for _ in range(4)),
            *(buffer(ROWS, BF16) for _ in range(4)),
            pltpu.SemaphoreType.DMA((2,)),
            pltpu.SemaphoreType.DMA((N_COPIES,)),
            pltpu.SemaphoreType.DMA((N_COPIES,)),
        ],
        compiler_params=pltpu.CompilerParams(
            collective_id=0, has_side_effects=True, vmem_limit_bytes=56 * 1024 * 1024
        ),
    )(scale.reshape(1), bias.reshape(1), protein, text)


def solution(mesh):
    in_specs = (P(("dp", "pair"), None), P(("dp", "pair"), None), P(), P())
    out_specs = (P(("dp", "pair"), None), P(("dp", "pair"), None))
    return jax.shard_map(on_device, mesh=mesh, in_specs=in_specs, out_specs=out_specs, check_vma=False)
```

```python
import math

import jax
import jax.numpy as jnp
from jax import lax
from jax.experimental import pallas as pl
from jax.experimental.pallas import tpu as pltpu
from jax.sharding import PartitionSpec as P

MESH = pl.DeviceIdType.MESH
F32, BF16 = jnp.float32, jnp.bfloat16
LOG2E = math.log2(math.e)
WIDTH = 1024
ROWS = 128
PARTS = ((0, 48), (48, 48), (96, 32))
PLACE = (0, 1, 2, 4, 3, 5, 6, 7)
N_COPIES = 114
TILE = (256, 256)


def neighbours():
    dp, pair = lax.axis_index("dp"), lax.axis_index("pair")
    z, x_lo, y = dp // 8, (dp // 4) % 2, dp % 4
    x_hi, core = pair // 2, pair % 2
    x = x_hi * 2 + x_lo

    def device(x, y, z, core):
        return (z * 8 + (x % 2) * 4 + y, (x // 2) * 2 + core)

    def p_flip(i):
        return i + 1 - 2 * (i % 2)

    def q_flip(i):
        return (i + 3 + 2 * (i % 2)) % 4

    def cube(flip):
        dy, dz = flip(y) - y, flip(z) - z
        return (
            device(flip(x), y, z, core),
            device(x, y + (1 - core) * dy, z + core * dz, core),
            device(x, y + core * dy, z + (1 - core) * dz, core),
        )

    return cube(p_flip), cube(q_flip), device(x, y, z, 1 - core)


def kernel(
    scale_ref, bias_ref, protein, text, out_p, out_q,
    unit_p, unit_q, norm_p, norm_q, rows_p, rows_q, coef, early_p, early_q, acc_p, acc_q, own_out, sib_out, sib_in,
    out1_p, out1_q, in1_p, in1_q, out2_p, out2_q, in2_p, in2_q, out3_p, out3_q, in3_p, in3_q,
    load_sem, send_sem, recv_sem,
):
    cube_p, cube_q, sibling = neighbours()
    barrier = pltpu.get_barrier_semaphore()
    for device in (*cube_p, *cube_q, sibling):
        pl.semaphore_signal(barrier, inc=1, device_id=device, device_id_type=MESH)
    load_p = pltpu.make_async_copy(protein, unit_p, load_sem.at[0])
    load_q = pltpu.make_async_copy(text, unit_q, load_sem.at[1])
    load_p.start()
    load_q.start()
    scale, bias = scale_ref[0], bias_ref[0]
    copies = []

    def send(src, dst, device):
        i = len(copies)
        copy = pltpu.make_async_remote_copy(
            src_ref=src, dst_ref=dst, send_sem=send_sem.at[i], recv_sem=recv_sem.at[i],
            device_id=device, device_id_type=MESH,
        )
        copy.start()
        copies.append(copy)
        return copy

    def normalise(load, unit, norm, rows):
        load.wait()
        values = unit[...]
        length = jnp.sqrt(jnp.sum(values * values, axis=1, keepdims=True) + 1e-06)
        values = values / length
        unit[...] = values
        norm[...] = length
        rows[0:ROWS, :] = values.astype(BF16)

    normalise(load_p, unit_p, norm_p, rows_p)
    normalise(load_q, unit_q, norm_q, rows_q)
    pl.semaphore_wait(barrier, 7)

    sides = ((rows_p, 2 * ROWS, cube_p), (rows_q, ROWS, cube_q))
    both = [(side, part) for part in range(3) for side in range(2)]
    arrival, from_sibling = {}, {}

    def pass_on(slot, link):
        for side, part in both:
            pass_part(side, part, slot, link)

    def pass_part(side, part, slot, link):
        rows, stride, cube = sides[side]
        start, size = PARTS[part]
        target = slot + (1 << link)
        arrival[side, part, target] = send(
            rows.at[pl.ds(PLACE[slot] * stride + start, size)],
            rows.at[pl.ds(PLACE[target] * stride + start, size)],
            cube[(part + link) % 3],
        )

    def to_sibling(place, start, size):
        row = place * 2 * ROWS + start
        from_sibling.setdefault(place, []).append(
            send(rows_p.at[pl.ds(row, size)], rows_p.at[pl.ds(row + ROWS, size)], sibling)
        )

    def receive(slot, links=(), sides=(0, 1)):
        for side in sides:
            for part in range(3):
                arrival[side, part, slot].wait_recv()
                for link in links[:1]:
                    pass_part(side, part, slot, link)
                if side == 0:
                    to_sibling(PLACE[slot], *PARTS[part])
            for link in links[1:]:
                for part in range(3):
                    pass_part(side, part, slot, link)

    def receive_sibling(*places):
        for place in places:
            for copy in from_sibling[place]:
                copy.wait_recv()

    slope, shift = scale * -LOG2E, bias * -LOG2E

    def dots(row, size, column, width):
        return lax.dot_general(
            rows_p[row : row + size, :], rows_q[column : column + width, :],
            (((1,), (1,)), ((), ())), preferred_element_type=F32,
        )

    def fill(row, end, column, last):
        for left in range(column, last, TILE[1]):
            for top in range(row, end, TILE[0]):
                power = jnp.exp2(dots(top, TILE[0], left, TILE[1]) * slope + shift)
                coef[top : top + TILE[0], left : left + TILE[1]] = (scale / (1.0 + power)).astype(BF16)

    def fill_own():
        values = dots(0, 4 * ROWS, 0, 2 * ROWS) * -slope - shift
        row = lax.broadcasted_iota(jnp.int32, values.shape, 0)
        column = lax.broadcasted_iota(jnp.int32, values.shape, 1)
        sign = jnp.where((row == column) & (row < ROWS), 1.0, -1.0)
        coef[0 : 4 * ROWS, 0 : 2 * ROWS] = (-sign * scale / (1.0 + jnp.exp2(sign * values))).astype(BF16)

    for link in range(3):
        pass_on(0, link)
    to_sibling(0, 0, ROWS)
    receive(1, (1, 2))
    receive(2, (2,))
    receive_sibling(0, 1)
    fill_own()
    receive(4)
    fill(0, 512, 256, 512)
    receive(3, (2,))
    receive_sibling(2, 3)
    fill(512, 1024, 0, 512)
    receive(5)
    def grad_p(place, start=0, end=8 * ROWS):
        row = place * 2 * ROWS
        return jnp.dot(coef[row : row + 2 * ROWS, start:end], rows_q[start:end, :], preferred_element_type=F32)

    def grad_q(place, start=0, end=16 * ROWS):
        return lax.dot_general(
            coef[start:end, place * ROWS : (place + 1) * ROWS], rows_p[start:end, :],
            (((0,), (0,)), ((), ())), preferred_element_type=F32,
        )

    sib_sums, sums = {}, {}

    def share(place, value):
        rows = pl.ds(place * ROWS, ROWS)
        sib_out[rows, :] = value[ROWS:]
        sib_sums[place] = send(sib_out.at[rows], sib_in.at[rows], sibling)
        own_out[rows, :] = value[:ROWS]

    def own_p(place):
        rows = pl.ds(place * ROWS, ROWS)
        sib_sums[place].wait_recv()
        return own_out[rows, :] + sib_in[rows, :]

    accs = (acc_p, acc_q)
    outs = ((out3_p, out2_p, out1_p), (out3_q, out2_q, out1_q))
    ins = ((in3_p, in2_p, in1_p), (in3_q, in2_q, in1_q))
    cubes = (cube_p, cube_q)

    def give(side, slot, part):
        link = slot.bit_length() - 1
        start, size = PARTS[part]
        rows = pl.ds((slot - (1 << link)) * ROWS + start, size)
        sums[side, slot, part] = send(
            outs[side][link].at[rows], ins[side][link].at[rows], cubes[side][(part + link) % 3]
        )

    def put(side, slot, value):
        link = slot.bit_length() - 1
        outs[side][link][pl.ds((slot - (1 << link)) * ROWS, ROWS), :] = value.astype(BF16)

    def give_all(side, slot):
        for part in range(3):
            give(side, slot, part)

    def total(side, slot, part):
        start, size = PARTS[part]
        rows = pl.ds(slot * ROWS + start, size)
        value = accs[side][rows, :]
        for link in (2, 1, 0):
            if slot < 1 << link:
                sums[side, slot + (1 << link), part].wait_recv()
                value += ins[side][link][rows, :].astype(F32)
        return value

    def add_and_give(side, slot):
        link = slot.bit_length() - 1
        for part, (start, size) in enumerate(PARTS):
            rows = pl.ds((slot - (1 << link)) * ROWS + start, size)
            outs[side][link][rows, :] = total(side, slot, part).astype(BF16)
            give(side, slot, part)

    def keep(side, slot, value):
        accs[side][pl.ds(slot * ROWS, ROWS), :] = value

    def give_p(slot):
        put(0, slot, own_p(PLACE[slot]))
        give_all(0, slot)

    def give_q(slot):
        put(1, slot, grad_q(PLACE[slot]))
        give_all(1, slot)

    def both_places(place, store_q):
        value = grad_p(place)
        store_q(grad_q(place))
        share(place, value)

    fill(0, 1024, 512, 768)
    receive_sibling(4)
    fill(1024, 1280, 0, 768)
    receive_sibling(5)
    fill(1280, 1536, 0, 768)
    receive(6)
    early_p[...] = grad_p(5, 0, 768)
    early_q[...] = grad_q(5, 0, 1536)
    receive_sibling(6)
    fill(1536, 1792, 0, 768)
    receive(7, sides=(0,))
    early_q[...] += grad_q(5, 1536, 1792)
    receive(7, sides=(1,))
    fill(1280, 1536, 768, 1024)
    share(5, early_p[...] + grad_p(5, 768, 1024))
    fill(0, 1024, 768, 1024)
    receive_sibling(7)
    fill(1792, 2048, 0, 1024)
    put(1, 5, early_q[...] + grad_q(5, 1792, 2048))
    give_all(1, 5)
    share(7, grad_p(7))
    give_p(5)
    fill(1024, 1280, 768, 1024)
    fill(1536, 1792, 768, 1024)
    give_q(7)
    give_p(7)
    share(6, grad_p(6))
    give_q(6)
    both_places(4, lambda value: keep(1, 3, value))
    give_p(6)
    both_places(3, lambda value: put(1, 4, value))
    keep(1, 2, grad_q(2))
    add_and_give(1, 3)
    give_all(1, 4)
    share(2, grad_p(2))
    keep(0, 3, own_p(4))
    add_and_give(0, 3)
    give_p(4)
    both_places(1, lambda value: keep(1, 1, value))
    add_and_give(1, 2)
    keep(0, 2, own_p(2))
    add_and_give(0, 2)
    both_places(0, lambda value: keep(1, 0, value))
    add_and_give(1, 1)
    keep(0, 1, own_p(1))
    keep(0, 0, own_p(0))
    add_and_give(0, 1)
    for side, unit, norm, out in ((1, unit_q, norm_q, out_q), (0, unit_p, norm_p, out_p)):
        for part, (start, size) in enumerate(PARTS):
            rows = pl.ds(start, size)
            grad = total(side, 0, part)
            direction = unit[rows, :]
            inner = jnp.sum(direction * grad, axis=1, keepdims=True)
            out[rows, :] = (grad - direction * inner) / norm[rows, :]
    for copy in copies:
        copy.wait_send()


def store(grad_p, grad_q, out_p, out_q, sem):
    copies = [
        pltpu.make_async_copy(grad_p, out_p, sem.at[0]),
        pltpu.make_async_copy(grad_q, out_q, sem.at[1]),
    ]
    for copy in copies:
        copy.start()
    for copy in copies:
        copy.wait()


def on_device(protein, text, scale, bias):
    def buffer(rows, kind):
        return pltpu.VMEM((rows, WIDTH), kind)

    result = pltpu.VMEM((ROWS, WIDTH), F32)
    grads = pl.pallas_call(
        kernel,
        out_shape=(result, result),
        in_specs=[pl.BlockSpec(memory_space=pltpu.SMEM)] * 2 + [pl.BlockSpec(memory_space=pl.ANY)] * 2,
        out_specs=[pl.BlockSpec(memory_space=pltpu.VMEM)] * 2,
        scratch_shapes=[
            buffer(ROWS, F32), buffer(ROWS, F32), pltpu.VMEM((ROWS, 1), F32), pltpu.VMEM((ROWS, 1), F32),
            buffer(2048, BF16), buffer(1024, BF16), buffer(2048, BF16),
            buffer(2 * ROWS, F32), buffer(ROWS, F32),
            *(buffer(4 * ROWS, F32) for _ in range(2)),
            *(buffer(8 * ROWS, F32) for _ in range(3)),
            *(buffer(4 * ROWS, BF16) for _ in range(4)),
            *(buffer(2 * ROWS, BF16) for _ in range(4)),
            *(buffer(ROWS, BF16) for _ in range(4)),
            pltpu.SemaphoreType.DMA((2,)),
            pltpu.SemaphoreType.DMA((N_COPIES,)),
            pltpu.SemaphoreType.DMA((N_COPIES,)),
        ],
        compiler_params=pltpu.CompilerParams(
            collective_id=0, has_side_effects=True, vmem_limit_bytes=56 * 1024 * 1024
        ),
    )(scale.reshape(1), bias.reshape(1), protein, text)
    return pl.pallas_call(
        store,
        out_shape=(jax.ShapeDtypeStruct((ROWS, WIDTH), F32),) * 2,
        in_specs=[pl.BlockSpec(memory_space=pl.ANY)] * 2,
        out_specs=[pl.BlockSpec(memory_space=pl.ANY)] * 2,
        scratch_shapes=[pltpu.SemaphoreType.DMA((2,))],
        compiler_params=pltpu.CompilerParams(vmem_limit_bytes=4 * 1024 * 1024),
    )(*grads)


def solution(mesh):
    in_specs = (P(("dp", "pair"), None), P(("dp", "pair"), None), P(), P())
    out_specs = (P(("dp", "pair"), None), P(("dp", "pair"), None))
    return jax.shard_map(on_device, mesh=mesh, in_specs=in_specs, out_specs=out_specs, check_vma=False)
```

```python
import math

import jax
import jax.numpy as jnp
from jax import lax
from jax.experimental import pallas as pl
from jax.experimental.pallas import tpu as pltpu
from jax.sharding import PartitionSpec as P

MESH = pl.DeviceIdType.MESH
F32, BF16 = jnp.float32, jnp.bfloat16
LOG2E = math.log2(math.e)
WIDTH = 1024
ROWS = 128
PARTS = ((0, 48), (48, 48), (96, 32))
PLACE = (0, 1, 2, 4, 3, 5, 6, 7)
N_COPIES = 114
TILE = (256, 256)


def neighbours():
    dp, pair = lax.axis_index("dp"), lax.axis_index("pair")
    z, x_lo, y = dp // 8, (dp // 4) % 2, dp % 4
    x_hi, core = pair // 2, pair % 2
    x = x_hi * 2 + x_lo

    def device(x, y, z, core):
        return (z * 8 + (x % 2) * 4 + y, (x // 2) * 2 + core)

    def p_flip(i):
        return i + 1 - 2 * (i % 2)

    def q_flip(i):
        return (i + 3 + 2 * (i % 2)) % 4

    def cube(flip):
        dy, dz = flip(y) - y, flip(z) - z
        return (
            device(flip(x), y, z, core),
            device(x, y + (1 - core) * dy, z + core * dz, core),
            device(x, y + core * dy, z + (1 - core) * dz, core),
        )

    return cube(p_flip), cube(q_flip), device(x, y, z, 1 - core)


def kernel(
    scale_ref, bias_ref, protein, text, out_p, out_q,
    unit_p, unit_q, norm_p, norm_q, rows_p, rows_q, coef, early_p, early_q, acc_p, acc_q, own_out, sib_out, sib_in,
    out1_p, out1_q, in1_p, in1_q, out2_p, out2_q, in2_p, in2_q, out3_p, out3_q, in3_p, in3_q,
    load_sem, send_sem, recv_sem,
):
    cube_p, cube_q, sibling = neighbours()
    barrier = pltpu.get_barrier_semaphore()
    for device in (*cube_p, *cube_q, sibling):
        pl.semaphore_signal(barrier, inc=1, device_id=device, device_id_type=MESH)
    load_p = pltpu.make_async_copy(protein, unit_p, load_sem.at[0])
    load_q = pltpu.make_async_copy(text, unit_q, load_sem.at[1])
    load_p.start()
    load_q.start()
    scale, bias = scale_ref[0], bias_ref[0]
    copies = []

    def send(src, dst, device):
        i = len(copies)
        copy = pltpu.make_async_remote_copy(
            src_ref=src, dst_ref=dst, send_sem=send_sem.at[i], recv_sem=recv_sem.at[i],
            device_id=device, device_id_type=MESH,
        )
        copy.start()
        copies.append(copy)
        return copy

    def normalise(load, unit, norm, rows):
        load.wait()
        values = unit[...]
        length = jnp.sqrt(jnp.sum(values * values, axis=1, keepdims=True) + 1e-06)
        values = values / length
        unit[...] = values
        norm[...] = length
        rows[0:ROWS, :] = values.astype(BF16)

    normalise(load_p, unit_p, norm_p, rows_p)
    normalise(load_q, unit_q, norm_q, rows_q)
    pl.semaphore_wait(barrier, 7)

    sides = ((rows_p, 2 * ROWS, cube_p), (rows_q, ROWS, cube_q))
    both = [(side, part) for part in range(3) for side in range(2)]
    arrival, from_sibling = {}, {}

    def pass_on(slot, link):
        for side, part in both:
            pass_part(side, part, slot, link)

    def pass_part(side, part, slot, link):
        rows, stride, cube = sides[side]
        start, size = PARTS[part]
        target = slot + (1 << link)
        arrival[side, part, target] = send(
            rows.at[pl.ds(PLACE[slot] * stride + start, size)],
            rows.at[pl.ds(PLACE[target] * stride + start, size)],
            cube[(part + link) % 3],
        )

    def to_sibling(place, start, size):
        row = place * 2 * ROWS + start
        from_sibling.setdefault(place, []).append(
            send(rows_p.at[pl.ds(row, size)], rows_p.at[pl.ds(row + ROWS, size)], sibling)
        )

    def receive(slot, links=(), sides=(0, 1)):
        for side in sides:
            for part in range(3):
                arrival[side, part, slot].wait_recv()
                for link in links[:1]:
                    pass_part(side, part, slot, link)
                if side == 0:
                    to_sibling(PLACE[slot], *PARTS[part])
            for link in links[1:]:
                for part in range(3):
                    pass_part(side, part, slot, link)

    def receive_sibling(*places):
        for place in places:
            for copy in from_sibling[place]:
                copy.wait_recv()

    slope, shift = scale * -LOG2E, bias * -LOG2E

    def dots(row, size, column, width):
        return lax.dot_general(
            rows_p[row : row + size, :], rows_q[column : column + width, :],
            (((1,), (1,)), ((), ())), preferred_element_type=F32,
        )

    def fill(row, end, column, last):
        for left in range(column, last, TILE[1]):
            for top in range(row, end, TILE[0]):
                power = jnp.exp2(dots(top, TILE[0], left, TILE[1]) * slope + shift)
                coef[top : top + TILE[0], left : left + TILE[1]] = (scale / (1.0 + power)).astype(BF16)

    def fill_own():
        values = dots(0, 4 * ROWS, 0, 2 * ROWS) * -slope - shift
        row = lax.broadcasted_iota(jnp.int32, values.shape, 0)
        column = lax.broadcasted_iota(jnp.int32, values.shape, 1)
        sign = jnp.where((row == column) & (row < ROWS), 1.0, -1.0)
        coef[0 : 4 * ROWS, 0 : 2 * ROWS] = (-sign * scale / (1.0 + jnp.exp2(sign * values))).astype(BF16)

    for link in range(3):
        pass_on(0, link)
    to_sibling(0, 0, ROWS)
    receive(1, (1, 2))
    receive(2, (2,))
    receive_sibling(0, 1)
    fill_own()
    receive(4)
    fill(0, 512, 256, 512)
    receive(3, (2,))
    receive_sibling(2, 3)
    fill(512, 1024, 0, 512)
    receive(5)
    def grad_p(place, start=0, end=8 * ROWS):
        row = place * 2 * ROWS
        return jnp.dot(coef[row : row + 2 * ROWS, start:end], rows_q[start:end, :], preferred_element_type=F32)

    def grad_q(place, start=0, end=16 * ROWS):
        return lax.dot_general(
            coef[start:end, place * ROWS : (place + 1) * ROWS], rows_p[start:end, :],
            (((0,), (0,)), ((), ())), preferred_element_type=F32,
        )

    sib_sums, sums = {}, {}

    def share(place, value):
        rows = pl.ds(place * ROWS, ROWS)
        sib_out[rows, :] = value[ROWS:]
        sib_sums[place] = send(sib_out.at[rows], sib_in.at[rows], sibling)
        own_out[rows, :] = value[:ROWS]

    def own_p(place):
        rows = pl.ds(place * ROWS, ROWS)
        sib_sums[place].wait_recv()
        return own_out[rows, :] + sib_in[rows, :]

    accs = (acc_p, acc_q)
    outs = ((out3_p, out2_p, out1_p), (out3_q, out2_q, out1_q))
    ins = ((in3_p, in2_p, in1_p), (in3_q, in2_q, in1_q))
    cubes = (cube_p, cube_q)

    def give(side, slot, part):
        link = slot.bit_length() - 1
        start, size = PARTS[part]
        rows = pl.ds((slot - (1 << link)) * ROWS + start, size)
        sums[side, slot, part] = send(
            outs[side][link].at[rows], ins[side][link].at[rows], cubes[side][(part + link) % 3]
        )

    def put(side, slot, value):
        link = slot.bit_length() - 1
        outs[side][link][pl.ds((slot - (1 << link)) * ROWS, ROWS), :] = value.astype(BF16)

    def give_all(side, slot):
        for part in range(3):
            give(side, slot, part)

    def total(side, slot, part):
        start, size = PARTS[part]
        rows = pl.ds(slot * ROWS + start, size)
        value = accs[side][rows, :]
        for link in (2, 1, 0):
            if slot < 1 << link:
                sums[side, slot + (1 << link), part].wait_recv()
                value += ins[side][link][rows, :].astype(F32)
        return value

    def add_and_give(side, slot):
        link = slot.bit_length() - 1
        for part, (start, size) in enumerate(PARTS):
            rows = pl.ds((slot - (1 << link)) * ROWS + start, size)
            outs[side][link][rows, :] = total(side, slot, part).astype(BF16)
            give(side, slot, part)

    def keep(side, slot, value):
        accs[side][pl.ds(slot * ROWS, ROWS), :] = value

    def give_p(slot):
        put(0, slot, own_p(PLACE[slot]))
        give_all(0, slot)

    def give_q(slot):
        put(1, slot, grad_q(PLACE[slot]))
        give_all(1, slot)

    def both_places(place, store_q):
        value = grad_p(place)
        store_q(grad_q(place))
        share(place, value)

    fill(0, 1024, 512, 768)
    receive_sibling(4)
    fill(1024, 1280, 0, 768)
    receive_sibling(5)
    fill(1280, 1536, 0, 768)
    receive(6)
    early_p[...] = grad_p(5, 0, 768)
    early_q[...] = grad_q(5, 0, 1536)
    receive_sibling(6)
    fill(1536, 1792, 0, 768)
    receive(7, sides=(0,))
    early_q[...] += grad_q(5, 1536, 1792)
    receive(7, sides=(1,))
    fill(1280, 1536, 768, 1024)
    share(5, early_p[...] + grad_p(5, 768, 1024))
    fill(0, 1024, 768, 1024)
    receive_sibling(7)
    fill(1792, 2048, 0, 1024)
    value = grad_p(7)
    put(1, 5, early_q[...] + grad_q(5, 1792, 2048))
    give_all(1, 5)
    share(7, value)
    give_p(5)
    fill(1024, 1280, 768, 1024)
    fill(1536, 1792, 768, 1024)
    give_q(7)
    give_p(7)
    share(6, grad_p(6))
    give_q(6)
    both_places(4, lambda value: keep(1, 3, value))
    give_p(6)
    both_places(3, lambda value: put(1, 4, value))
    keep(1, 2, grad_q(2))
    add_and_give(1, 3)
    give_all(1, 4)
    share(2, grad_p(2))
    keep(0, 3, own_p(4))
    add_and_give(0, 3)
    give_p(4)
    both_places(1, lambda value: keep(1, 1, value))
    add_and_give(1, 2)
    keep(0, 2, own_p(2))
    add_and_give(0, 2)
    both_places(0, lambda value: keep(1, 0, value))
    add_and_give(1, 1)
    keep(0, 1, own_p(1))
    keep(0, 0, own_p(0))
    add_and_give(0, 1)
    for side, unit, norm, out in ((0, unit_p, norm_p, out_p), (1, unit_q, norm_q, out_q)):
        for part, (start, size) in enumerate(PARTS):
            rows = pl.ds(start, size)
            grad = total(side, 0, part)
            direction = unit[rows, :]
            inner = jnp.sum(direction * grad, axis=1, keepdims=True)
            out[rows, :] = (grad - direction * inner) / norm[rows, :]
    for copy in copies:
        copy.wait_send()


def store(grad_p, grad_q, out_p, out_q, sem):
    copies = [
        pltpu.make_async_copy(grad_p, out_p, sem.at[0]),
        pltpu.make_async_copy(grad_q, out_q, sem.at[1]),
    ]
    for copy in copies:
        copy.start()
    for copy in copies:
        copy.wait()


def on_device(protein, text, scale, bias):
    def buffer(rows, kind):
        return pltpu.VMEM((rows, WIDTH), kind)

    result = pltpu.VMEM((ROWS, WIDTH), F32)
    grads = pl.pallas_call(
        kernel,
        out_shape=(result, result),
        in_specs=[pl.BlockSpec(memory_space=pltpu.SMEM)] * 2 + [pl.BlockSpec(memory_space=pl.ANY)] * 2,
        out_specs=[pl.BlockSpec(memory_space=pltpu.VMEM)] * 2,
        scratch_shapes=[
            buffer(ROWS, F32), buffer(ROWS, F32), pltpu.VMEM((ROWS, 1), F32), pltpu.VMEM((ROWS, 1), F32),
            buffer(2048, BF16), buffer(1024, BF16), buffer(2048, BF16),
            buffer(2 * ROWS, F32), buffer(ROWS, F32),
            *(buffer(4 * ROWS, F32) for _ in range(2)),
            *(buffer(8 * ROWS, F32) for _ in range(3)),
            *(buffer(4 * ROWS, BF16) for _ in range(4)),
            *(buffer(2 * ROWS, BF16) for _ in range(4)),
            *(buffer(ROWS, BF16) for _ in range(4)),
            pltpu.SemaphoreType.DMA((2,)),
            pltpu.SemaphoreType.DMA((N_COPIES,)),
            pltpu.SemaphoreType.DMA((N_COPIES,)),
        ],
        compiler_params=pltpu.CompilerParams(
            collective_id=0, has_side_effects=True, vmem_limit_bytes=56 * 1024 * 1024
        ),
    )(scale.reshape(1), bias.reshape(1), protein, text)
    return pl.pallas_call(
        store,
        out_shape=(jax.ShapeDtypeStruct((ROWS, WIDTH), F32),) * 2,
        in_specs=[pl.BlockSpec(memory_space=pl.ANY)] * 2,
        out_specs=[pl.BlockSpec(memory_space=pl.ANY)] * 2,
        scratch_shapes=[pltpu.SemaphoreType.DMA((2,))],
        compiler_params=pltpu.CompilerParams(vmem_limit_bytes=4 * 1024 * 1024),
    )(*grads)


def solution(mesh):
    in_specs = (P(("dp", "pair"), None), P(("dp", "pair"), None), P(), P())
    out_specs = (P(("dp", "pair"), None), P(("dp", "pair"), None))
    return jax.shard_map(on_device, mesh=mesh, in_specs=in_specs, out_specs=out_specs, check_vma=False)
```

```python
import math

import jax
import jax.numpy as jnp
from jax import lax
from jax.experimental import pallas as pl
from jax.experimental.pallas import tpu as pltpu
from jax.sharding import PartitionSpec as P

MESH = pl.DeviceIdType.MESH
F32, BF16 = jnp.float32, jnp.bfloat16
LOG2E = math.log2(math.e)
WIDTH = 1024
ROWS = 128
PARTS = ((0, 48), (48, 48), (96, 32))
PLACE = (0, 1, 2, 4, 3, 5, 6, 7)
N_COPIES = 114
TILE = (256, 256)


def neighbours():
    dp, pair = lax.axis_index("dp"), lax.axis_index("pair")
    z, x_lo, y = dp // 8, (dp // 4) % 2, dp % 4
    x_hi, core = pair // 2, pair % 2
    x = x_hi * 2 + x_lo

    def device(x, y, z, core):
        return (z * 8 + (x % 2) * 4 + y, (x // 2) * 2 + core)

    def p_flip(i):
        return i + 1 - 2 * (i % 2)

    def q_flip(i):
        return (i + 3 + 2 * (i % 2)) % 4

    def cube(flip):
        dy, dz = flip(y) - y, flip(z) - z
        return (
            device(flip(x), y, z, core),
            device(x, y + (1 - core) * dy, z + core * dz, core),
            device(x, y + core * dy, z + (1 - core) * dz, core),
        )

    return cube(p_flip), cube(q_flip), device(x, y, z, 1 - core)


def kernel(
    scale_ref, bias_ref, protein, text, out_p, out_q,
    unit_p, unit_q, norm_p, norm_q, rows_p, rows_q, coef, early_p, early_q, acc_p, acc_q, own_out, sib_out, sib_in,
    out1_p, out1_q, in1_p, in1_q, out2_p, out2_q, in2_p, in2_q, out3_p, out3_q, in3_p, in3_q,
    load_sem, send_sem, recv_sem,
):
    cube_p, cube_q, sibling = neighbours()
    barrier = pltpu.get_barrier_semaphore()
    for device in (*cube_p, *cube_q, sibling):
        pl.semaphore_signal(barrier, inc=1, device_id=device, device_id_type=MESH)
    load_p = pltpu.make_async_copy(protein, unit_p, load_sem.at[0])
    load_q = pltpu.make_async_copy(text, unit_q, load_sem.at[1])
    load_p.start()
    load_q.start()
    scale, bias = scale_ref[0], bias_ref[0]
    copies = []

    def send(src, dst, device):
        i = len(copies)
        copy = pltpu.make_async_remote_copy(
            src_ref=src, dst_ref=dst, send_sem=send_sem.at[i], recv_sem=recv_sem.at[i],
            device_id=device, device_id_type=MESH,
        )
        copy.start()
        copies.append(copy)
        return copy

    def normalise(load, unit, norm, rows):
        load.wait()
        values = unit[...]
        length = jnp.sqrt(jnp.sum(values * values, axis=1, keepdims=True) + 1e-06)
        values = values / length
        unit[...] = values
        norm[...] = length
        rows[0:ROWS, :] = values.astype(BF16)

    normalise(load_p, unit_p, norm_p, rows_p)
    normalise(load_q, unit_q, norm_q, rows_q)
    pl.semaphore_wait(barrier, 7)

    sides = ((rows_p, 2 * ROWS, cube_p), (rows_q, ROWS, cube_q))
    both = [(side, part) for part in range(3) for side in range(2)]
    arrival, from_sibling = {}, {}

    def pass_on(slot, link):
        for side, part in both:
            pass_part(side, part, slot, link)

    def pass_part(side, part, slot, link):
        rows, stride, cube = sides[side]
        start, size = PARTS[part]
        target = slot + (1 << link)
        arrival[side, part, target] = send(
            rows.at[pl.ds(PLACE[slot] * stride + start, size)],
            rows.at[pl.ds(PLACE[target] * stride + start, size)],
            cube[(part + link) % 3],
        )

    def to_sibling(place, start, size):
        row = place * 2 * ROWS + start
        from_sibling.setdefault(place, []).append(
            send(rows_p.at[pl.ds(row, size)], rows_p.at[pl.ds(row + ROWS, size)], sibling)
        )

    def receive(slot, links=(), sides=(0, 1)):
        for side in sides:
            for part in range(3):
                arrival[side, part, slot].wait_recv()
                for link in links[:1]:
                    pass_part(side, part, slot, link)
                if side == 0:
                    to_sibling(PLACE[slot], *PARTS[part])
            for link in links[1:]:
                for part in range(3):
                    pass_part(side, part, slot, link)

    def receive_sibling(*places):
        for place in places:
            for copy in from_sibling[place]:
                copy.wait_recv()

    slope, shift = scale * -LOG2E, bias * -LOG2E

    def dots(row, size, column, width):
        return lax.dot_general(
            rows_p[row : row + size, :], rows_q[column : column + width, :],
            (((1,), (1,)), ((), ())), preferred_element_type=F32,
        )

    def fill(row, end, column, last):
        for left in range(column, last, TILE[1]):
            for top in range(row, end, TILE[0]):
                power = jnp.exp2(dots(top, TILE[0], left, TILE[1]) * slope + shift)
                coef[top : top + TILE[0], left : left + TILE[1]] = (scale / (1.0 + power)).astype(BF16)

    def fill_own():
        values = dots(0, 4 * ROWS, 0, 2 * ROWS) * -slope - shift
        row = lax.broadcasted_iota(jnp.int32, values.shape, 0)
        column = lax.broadcasted_iota(jnp.int32, values.shape, 1)
        sign = jnp.where((row == column) & (row < ROWS), 1.0, -1.0)
        coef[0 : 4 * ROWS, 0 : 2 * ROWS] = (-sign * scale / (1.0 + jnp.exp2(sign * values))).astype(BF16)

    for link in range(3):
        pass_on(0, link)
    to_sibling(0, 0, ROWS)
    receive(1, (1, 2))
    receive(2, (2,))
    receive_sibling(0, 1)
    fill_own()
    receive(4)
    fill(0, 512, 256, 512)
    receive(3, (2,))
    receive_sibling(2, 3)
    fill(512, 1024, 0, 512)
    receive(5)
    def grad_p(place, start=0, end=8 * ROWS):
        row = place * 2 * ROWS
        return jnp.dot(coef[row : row + 2 * ROWS, start:end], rows_q[start:end, :], preferred_element_type=F32)

    def grad_q(place, start=0, end=16 * ROWS):
        return lax.dot_general(
            coef[start:end, place * ROWS : (place + 1) * ROWS], rows_p[start:end, :],
            (((0,), (0,)), ((), ())), preferred_element_type=F32,
        )

    sib_sums, sums = {}, {}

    def share(place, value):
        rows = pl.ds(place * ROWS, ROWS)
        sib_out[rows, :] = value[ROWS:]
        sib_sums[place] = send(sib_out.at[rows], sib_in.at[rows], sibling)
        own_out[rows, :] = value[:ROWS]

    def own_p(place):
        rows = pl.ds(place * ROWS, ROWS)
        sib_sums[place].wait_recv()
        return own_out[rows, :] + sib_in[rows, :]

    accs = (acc_p, acc_q)
    outs = ((out3_p, out2_p, out1_p), (out3_q, out2_q, out1_q))
    ins = ((in3_p, in2_p, in1_p), (in3_q, in2_q, in1_q))
    cubes = (cube_p, cube_q)

    def give(side, slot, part):
        link = slot.bit_length() - 1
        start, size = PARTS[part]
        rows = pl.ds((slot - (1 << link)) * ROWS + start, size)
        sums[side, slot, part] = send(
            outs[side][link].at[rows], ins[side][link].at[rows], cubes[side][(part + link) % 3]
        )

    def put(side, slot, value):
        link = slot.bit_length() - 1
        outs[side][link][pl.ds((slot - (1 << link)) * ROWS, ROWS), :] = value.astype(BF16)

    def give_all(side, slot):
        for part in range(3):
            give(side, slot, part)

    def total(side, slot, part):
        start, size = PARTS[part]
        rows = pl.ds(slot * ROWS + start, size)
        value = accs[side][rows, :]
        for link in (2, 1, 0):
            if slot < 1 << link:
                sums[side, slot + (1 << link), part].wait_recv()
                value += ins[side][link][rows, :].astype(F32)
        return value

    def add_and_give(side, slot):
        link = slot.bit_length() - 1
        for part, (start, size) in enumerate(PARTS):
            rows = pl.ds((slot - (1 << link)) * ROWS + start, size)
            outs[side][link][rows, :] = total(side, slot, part).astype(BF16)
            give(side, slot, part)

    def keep(side, slot, value):
        accs[side][pl.ds(slot * ROWS, ROWS), :] = value

    def give_p(slot):
        put(0, slot, own_p(PLACE[slot]))
        give_all(0, slot)

    def give_q(slot):
        put(1, slot, grad_q(PLACE[slot]))
        give_all(1, slot)

    def both_places(place, store_q):
        value = grad_p(place)
        store_q(grad_q(place))
        share(place, value)

    fill(0, 1024, 512, 768)
    receive_sibling(4)
    fill(1024, 1280, 0, 768)
    receive_sibling(5)
    fill(1280, 1536, 0, 768)
    receive(6)
    early_p[...] = grad_p(5, 0, 768)
    early_q[...] = grad_q(5, 0, 1536)
    receive_sibling(6)
    fill(1536, 1792, 0, 768)
    receive(7, sides=(0,))
    early_q[...] += grad_q(5, 1536, 1792)
    receive(7, sides=(1,))
    fill(1280, 1536, 768, 1024)
    share(5, early_p[...] + grad_p(5, 768, 1024))
    fill(0, 1024, 768, 1024)
    receive_sibling(7)
    fill(1792, 2048, 0, 1024)
    value = grad_p(7)
    put(1, 5, early_q[...] + grad_q(5, 1792, 2048))
    give_all(1, 5)
    share(7, value)
    give_p(5)
    fill(1024, 1280, 768, 1024)
    fill(1536, 1792, 768, 1024)
    give_q(7)
    give_p(7)
    share(6, grad_p(6))
    give_q(6)
    both_places(4, lambda value: keep(1, 3, value))
    give_p(6)
    both_places(3, lambda value: put(1, 4, value))
    keep(1, 2, grad_q(2))
    add_and_give(1, 3)
    give_all(1, 4)
    share(2, grad_p(2))
    keep(0, 3, own_p(4))
    add_and_give(0, 3)
    give_p(4)
    both_places(1, lambda value: keep(1, 1, value))
    add_and_give(1, 2)
    keep(0, 2, own_p(2))
    add_and_give(0, 2)
    both_places(0, lambda value: keep(1, 0, value))
    add_and_give(1, 1)
    keep(0, 1, own_p(1))
    add_and_give(0, 1)
    keep(0, 0, own_p(0))
    for side, unit, norm, out in ((0, unit_p, norm_p, out_p), (1, unit_q, norm_q, out_q)):
        for part, (start, size) in enumerate(PARTS):
            rows = pl.ds(start, size)
            grad = total(side, 0, part)
            direction = unit[rows, :]
            inner = jnp.sum(direction * grad, axis=1, keepdims=True)
            out[rows, :] = (grad - direction * inner) / norm[rows, :]
    for copy in copies:
        copy.wait_send()


def store(grad_p, grad_q, out_p, out_q, sem):
    copies = [
        pltpu.make_async_copy(grad_p, out_p, sem.at[0]),
        pltpu.make_async_copy(grad_q, out_q, sem.at[1]),
    ]
    for copy in copies:
        copy.start()
    for copy in copies:
        copy.wait()


def on_device(protein, text, scale, bias):
    def buffer(rows, kind):
        return pltpu.VMEM((rows, WIDTH), kind)

    result = pltpu.VMEM((ROWS, WIDTH), F32)
    grads = pl.pallas_call(
        kernel,
        out_shape=(result, result),
        in_specs=[pl.BlockSpec(memory_space=pltpu.SMEM)] * 2 + [pl.BlockSpec(memory_space=pl.ANY)] * 2,
        out_specs=[pl.BlockSpec(memory_space=pltpu.VMEM)] * 2,
        scratch_shapes=[
            buffer(ROWS, F32), buffer(ROWS, F32), pltpu.VMEM((ROWS, 1), F32), pltpu.VMEM((ROWS, 1), F32),
            buffer(2048, BF16), buffer(1024, BF16), buffer(2048, BF16),
            buffer(2 * ROWS, F32), buffer(ROWS, F32),
            *(buffer(4 * ROWS, F32) for _ in range(2)),
            *(buffer(8 * ROWS, F32) for _ in range(3)),
            *(buffer(4 * ROWS, BF16) for _ in range(4)),
            *(buffer(2 * ROWS, BF16) for _ in range(4)),
            *(buffer(ROWS, BF16) for _ in range(4)),
            pltpu.SemaphoreType.DMA((2,)),
            pltpu.SemaphoreType.DMA((N_COPIES,)),
            pltpu.SemaphoreType.DMA((N_COPIES,)),
        ],
        compiler_params=pltpu.CompilerParams(
            collective_id=0, has_side_effects=True, vmem_limit_bytes=56 * 1024 * 1024
        ),
    )(scale.reshape(1), bias.reshape(1), protein, text)
    return pl.pallas_call(
        store,
        out_shape=(jax.ShapeDtypeStruct((ROWS, WIDTH), F32),) * 2,
        in_specs=[pl.BlockSpec(memory_space=pl.ANY)] * 2,
        out_specs=[pl.BlockSpec(memory_space=pl.ANY)] * 2,
        scratch_shapes=[pltpu.SemaphoreType.DMA((2,))],
        compiler_params=pltpu.CompilerParams(vmem_limit_bytes=4 * 1024 * 1024),
    )(*grads)


def solution(mesh):
    in_specs = (P(("dp", "pair"), None), P(("dp", "pair"), None), P(), P())
    out_specs = (P(("dp", "pair"), None), P(("dp", "pair"), None))
    return jax.shard_map(on_device, mesh=mesh, in_specs=in_specs, out_specs=out_specs, check_vma=False)
```
